512 devices in a mesh: half: 2 (over core), grp: 8 (over y), dev: 32 (over z, x).
Axes of the slice: x: 4, y: 8, z: 8, core: 2. Of those that a mesh axis runs over, the one named last changes fastest.
Arguments:
- panel_block: float32 [16384, 512], P(('half', 'grp', 'dev')), may hold values from -1 to 1, as said below
- trailing: float32 [16384, 4096], P(('half', 'grp'), 'dev'), may hold values from -6 to 6
Outputs:
- triangle: float32 [512, 512], replicated
- projected: float32 [512, 4096], P(None, 'dev')
- remainder: float32 [16384, 4096], P(('half', 'grp'), 'dev')
The draws below stay inside these ranges and needn't reach their ends.
Inputs may be any that keep to these rules, and one draw needn't show every extreme that they name: `panel_block`: of full column rank.
All inputs are finite; a program needn't handle non-finite values.
Results may differ from the reference program's by a relative error of at most 0.0003.
Values sent between devices are 32-bit elements; how exact they have to be, the bound alone decides.
No kernel may reach another device: no remote copies, remote signals or barrier semaphores. Data moves between devices by JAX's collectives and lax.ppermute only.
A program may use at most 64 MiB of HBM per device.

```python
import jax
import jax.numpy as jnp
from jax import lax

P_SIZE = 512
ROWS = 16384
SLAB = 4096


def draw_panel_block(key, part):
    first = jax.random.fold_in(key, 11)
    second = jax.random.fold_in(key, 23)
    values = jnp.clip(jax.random.normal(first, (ROWS, P_SIZE), jnp.float32), -6.0, 6.0)
    position = jnp.arange(ROWS, dtype=jnp.float32) / ROWS
    row_scale = (3.0 ** position)[:, None] * jax.random.uniform(second, (ROWS, 1), jnp.float32, 0.7, 1.3)
    values = values * row_scale / jnp.sqrt(jnp.float32(ROWS))
    return jnp.clip(values, -1.0, 1.0)


def block_scale(rng, extent, split, least, largest):
    factor_of = 1.0
    for dim, blocks in split:
        steps = jax.random.uniform(jax.random.fold_in(jax.random.fold_in(rng, 6), dim), (blocks,), jnp.float32, least / len(split), largest / len(split))
        factor_of = factor_of * jnp.repeat(jnp.exp(steps), extent[dim] // blocks).reshape((-1,) + (1,) * (len(extent) - 1 - dim))
    return factor_of


def normal_values(stream_key, extent, width, limit, pieces=(), kind=jnp.bfloat16):
    gain = block_scale(stream_key, extent, pieces, -0.22, 0.18) if pieces else 1.0
    values = jax.random.normal(stream_key, extent, jnp.float32) * width * gain
    return jnp.minimum(jnp.maximum(values, -limit), limit).astype(kind)


def setup_inputs(seed: int = 0) -> dict:
    arg_keys = jax.random.split(jax.random.key(seed), 3)
    panel_block = draw_panel_block(jax.random.fold_in(arg_keys[2], 71), 0)
    trailing = normal_values(arg_keys[1], (ROWS, SLAB), 1.0, 6.0, ((0, 16), (1, 32)), jnp.float32)
    return {"panel_block": panel_block, "trailing": trailing}


def reference(panel_block, trailing):
    orthonormal, upper_part = jnp.linalg.qr(panel_block)
    signs = jnp.sign(jnp.diagonal(upper_part))
    triangle = upper_part * signs[:, None]
    orthonormal = orthonormal * signs[None, :]
    projected = jnp.dot(orthonormal.T, trailing, precision=lax.Precision.HIGHEST)
    remainder = trailing - jnp.dot(orthonormal, projected, precision=lax.Precision.HIGHEST)
    return (triangle, projected, remainder)
```

```python
import jax
import jax.numpy as jnp
from jax import lax
from jax.experimental import pallas as pl
from jax.experimental.pallas import tpu as pltpu
from jax.sharding import PartitionSpec as P

N = 512
B = 128
V = 8
NB = N // B
NP = B // V
HI = lax.Precision.HIGHEST
F32 = jnp.float32


def across_lanes(v, c):
    return jnp.broadcast_to(v[:, c : c + 1], (V, B))


def across_rows(v, j):
    return jnp.broadcast_to(v[j : j + 1, :], (V, B))


def factor_block(m):
    row = lax.broadcasted_iota(jnp.int32, (V, B), 0)
    lane = lax.broadcasted_iota(jnp.int32, (V, B), 1)
    ups, invs = [], []
    for p in range(NP):
        r0 = p * V
        mp = m[p]
        diag = (lane >= r0) & (lane < r0 + V)
        eye = (lane == row + r0).astype(F32)
        b = [across_lanes(mp, r0 + j) for j in range(V)]
        low, low_e, full = mp, eye, jnp.where(diag, eye, mp)
        dv = jnp.ones((V, B), F32)
        for j in range(V):
            d = across_rows(b[j], j)
            dv = jnp.where(row == j, d, dv)
            mult = b[j] * (1.0 / d)
            mfull = jnp.where(row == j, 0.0, mult)
            mlow = jnp.where(row > j, mult, 0.0)
            for k in range(j + 1, V):
                b[k] = b[k] - mfull * across_rows(b[k], j)
            low = low - mlow * across_rows(low, j)
            low_e = low_e - mlow * across_rows(low_e, j)
            full = full - mfull * across_rows(full, j)
        rs = lax.rsqrt(dv)
        full = full * (1.0 / dv)
        ups.append(jnp.where(lane >= row + r0, low * rs, 0.0))
        invs.append(jnp.where(lane <= row + r0, jnp.where(diag, low_e, low) * rs, 0.0))
        if p + 1 < NP:
            f = [across_rows(full, j) for j in range(V)]
            for q in range(p + 1, NP):
                old = m[q]
                t = [across_lanes(old, r0 + j) * f[j] for j in range(V)]
                s = ((t[0] + t[1]) + (t[2] + t[3])) + ((t[4] + t[5]) + (t[6] + t[7]))
                m[q] = jnp.where(diag, 0.0, old) - s
    return jnp.concatenate(ups, 0), jnp.concatenate(invs, 0)


def mm(a, b, dims=((1,), (0,))):
    return lax.dot_general(a, b, (dims, ((), ())), precision=HI, preferred_element_type=F32)


def factor_kernel(g_ref, r_ref, w_ref, m_ref):
    m_ref[...] = g_ref[...]
    r_ref[...] = jnp.zeros_like(r_ref)
    for k in range(NB):
        o = k * B
        e = o + B
        u, v = factor_block([m_ref[o + V * i : o + V * (i + 1), o:e] for i in range(NP)])
        r_ref[o:e, o:e] = u
        w_ref[o:e, o:e] = v
        if k:
            w_ref[o:e, :o] = mm(v, m_ref[o:e, :o])
        if k + 1 < NB:
            w_ref[o:e, e:] = jnp.zeros((B, N - e), F32)
            ps = mm(v, m_ref[o:e, e:])
            r_ref[o:e, e:] = ps
            lt = mm(m_ref[e:, o:e], v, ((1,), (1,)))
            m_ref[e:, e:] = m_ref[e:, e:] - mm(lt, ps)
            if k:
                m_ref[e:, :o] = m_ref[e:, :o] - mm(lt, w_ref[o:e, :o])
            m_ref[e:, o:e] = -mm(lt, v)


def factor(gram):
    out = jax.ShapeDtypeStruct((N, N), F32)
    vmem = pl.BlockSpec(memory_space=pltpu.VMEM)
    return pl.pallas_call(
        factor_kernel,
        out_shape=(out, out),
        scratch_shapes=[pltpu.VMEM((N, N), F32)],
        in_specs=[vmem],
        out_specs=(vmem, vmem),
        compiler_params=pltpu.CompilerParams(vmem_limit_bytes=32 * 2**20),
        name="factor",
    )(gram)


def sent_to_all(x, axis):
    size = lax.axis_size(axis)
    return lax.all_to_all(jnp.broadcast_to(x[None], (size, *x.shape)), axis, 0, 0, tiled=True)


def summed(x, axis):
    size = lax.axis_size(axis)
    rows = x.shape[0] // size
    share = lax.all_to_all(x.reshape(size, rows, x.shape[1]), axis, 0, 0, tiled=True).sum(0)
    return sent_to_all(share, axis).reshape(x.shape)


def on_device(panel_block, trailing):
    panel_group = sent_to_all(panel_block, "dev").reshape(-1, N)
    gram_part = jnp.dot(panel_group.T, panel_group, precision=HI)
    cross_part = jnp.dot(panel_group.T, trailing, precision=HI)
    total = summed(jnp.concatenate([gram_part, cross_part], 1), ("half", "grp"))
    triangle, inverse = factor(total[:, :N])
    projected = jnp.dot(inverse, total[:, N:], precision=HI)
    solved = jnp.dot(inverse.T, projected, precision=HI)
    remainder = trailing - jnp.dot(panel_group, solved, precision=HI)
    return (triangle, projected, remainder)


def solution(mesh):
    placed = (P(("half", "grp", "dev"), None), P(("half", "grp"), "dev"))
    return jax.shard_map(
        on_device,
        mesh=mesh,
        in_specs=placed,
        out_specs=(P(), P(None, "dev"), P(("half", "grp"), "dev")),
        check_vma=False,
    )
```

```python
import jax
import jax.numpy as jnp
from jax import lax
from jax.experimental import pallas as pl
from jax.experimental.pallas import tpu as pltpu
from jax.sharding import PartitionSpec as P

N = 512
B = 128
V = 8
NB = N // B
NP = B // V
X = 4
Z = 8
SHARE_ROWS = B // X
HI = lax.Precision.HIGHEST
F32 = jnp.float32


def across_lanes(v, c):
    return jnp.broadcast_to(v[:, c : c + 1], (V, B))


def across_rows(v, j):
    return jnp.broadcast_to(v[j : j + 1, :], (V, B))


def factor_block(m):
    row = lax.broadcasted_iota(jnp.int32, (V, B), 0)
    lane = lax.broadcasted_iota(jnp.int32, (V, B), 1)
    ups, invs = [], []
    for p in range(NP):
        r0 = p * V
        mp = m[p]
        diag = (lane >= r0) & (lane < r0 + V)
        eye = (lane == row + r0).astype(F32)
        b = [across_lanes(mp, r0 + j) for j in range(V)]
        low, low_e, full = mp, eye, jnp.where(diag, eye, mp)
        dv = jnp.ones((V, B), F32)
        for j in range(V):
            d = across_rows(b[j], j)
            dv = jnp.where(row == j, d, dv)
            mult = b[j] * (1.0 / d)
            mfull = jnp.where(row == j, 0.0, mult)
            mlow = jnp.where(row > j, mult, 0.0)
            for k in range(j + 1, V):
                b[k] = b[k] - mfull * across_rows(b[k], j)
            low = low - mlow * across_rows(low, j)
            low_e = low_e - mlow * across_rows(low_e, j)
            full = full - mfull * across_rows(full, j)
        rs = lax.rsqrt(dv)
        full = full * (1.0 / dv)
        ups.append(jnp.where(lane >= row + r0, low * rs, 0.0))
        invs.append(jnp.where(lane <= row + r0, jnp.where(diag, low_e, low) * rs, 0.0))
        if p + 1 < NP:
            f = [across_rows(full, j) for j in range(V)]
            for q in range(p + 1, NP):
                old = m[q]
                t = [across_lanes(old, r0 + j) * f[j] for j in range(V)]
                s = ((t[0] + t[1]) + (t[2] + t[3])) + ((t[4] + t[5]) + (t[6] + t[7]))
                m[q] = jnp.where(diag, 0.0, old) - s
    return jnp.concatenate(ups, 0), jnp.concatenate(invs, 0)


def mm(a, b, dims=((1,), (0,))):
    return lax.dot_general(a, b, (dims, ((), ())), precision=HI, preferred_element_type=F32)


def tile(g_ref, block, t):
    s = block * SHARE_ROWS + (t % 4) * V
    return g_ref[s // 40 * 4 + t // 4, s % 40 : s % 40 + V, :]


def factor_kernel(g_ref, r_ref, w_ref, end_ref, m_ref):
    block = 0
    for i in range(NB):
        for j in range(i, NB):
            for t in range(NP):
                m_ref[i * B + V * t : i * B + V * (t + 1), j * B : (j + 1) * B] = tile(g_ref, block, t)
            block += 1
    r_ref[...] = jnp.zeros_like(r_ref)
    for k in range(NB):
        o = k * B
        e = o + B
        u, v = factor_block([m_ref[o + V * i : o + V * (i + 1), o:e] for i in range(NP)])
        r_ref[o:e, o:e] = u
        w_ref[o:e, o:e] = v
        if k:
            w_ref[o:e, :o] = mm(v, m_ref[o:e, :o])
        if k + 1 < NB:
            w_ref[o:e, e:] = jnp.zeros((B, N - e), F32)
            ps = mm(v, m_ref[o:e, e:])
            r_ref[o:e, e:] = ps
            for i in range(k + 1, NB):
                q, lt = i * B, ps[:, (i - k - 1) * B : (i - k) * B].T
                m_ref[q : q + B, q:] = m_ref[q : q + B, q:] - mm(lt, ps[:, q - e :])
                if k:
                    m_ref[q : q + B, :o] = m_ref[q : q + B, :o] - mm(lt, w_ref[o:e, :o])
                m_ref[q : q + B, o:e] = -mm(lt, v)
    end_ref[...] = jnp.zeros_like(end_ref)


def factor(shares):
    out = jax.ShapeDtypeStruct((N, N), F32)
    vmem = pl.BlockSpec(memory_space=pltpu.VMEM)
    return pl.pallas_call(
        factor_kernel,
        out_shape=(out, out, jax.ShapeDtypeStruct((V, B), F32)),
        scratch_shapes=[pltpu.VMEM((N, N), F32)],
        in_specs=[vmem],
        out_specs=(vmem, vmem, vmem),
        compiler_params=pltpu.CompilerParams(vmem_limit_bytes=32 * 2**20),
        cost_estimate=pl.CostEstimate(flops=20_000_000_000, bytes_accessed=3 * 2**20, transcendentals=0),
        name="factor",
    )(shares)


def sent_to_all(x, axis, groups=None):
    size = len(groups[0]) if groups else lax.axis_size(axis)
    copies = jnp.broadcast_to(x[None], (size, *x.shape))
    return lax.all_to_all(copies, axis, 0, 0, axis_index_groups=groups, tiled=True)


def swapped(x):
    return lax.ppermute(x, "half", [(0, 1), (1, 0)])


def gram_kernel(p_ref, own_ref, g_ref):
    first = lax.axis_index("dev") % X * SHARE_ROWS
    block = 0
    for i in range(NB):
        g_ref[:, i * B :] = mm(p_ref[:, i * B : (i + 1) * B], p_ref[:, i * B :], ((0,), (0,)))
        for j in range(i, NB):
            for t in range(SHARE_ROWS // V):
                s = block * SHARE_ROWS + t * V
                row = pl.multiple_of(first + t * V, V)
                own_ref[s // 40, s % 40 : s % 40 + V, :] = g_ref[pl.ds(row, V), j * B : (j + 1) * B]
            block += 1


def gram_shares(rows):
    vmem = pl.BlockSpec(memory_space=pltpu.VMEM)
    return pl.pallas_call(
        gram_kernel,
        out_shape=jax.ShapeDtypeStruct((Z, 40, B), F32),
        scratch_shapes=[pltpu.VMEM((B, N), F32)],
        in_specs=[vmem],
        out_specs=vmem,
        name="gram",
    )(rows)


def finish_kernel(w_ref, kept_ref, other_ref, p_ref, t_ref, y_ref, r_ref):
    first = lax.axis_index("half") == 0
    kept, other = kept_ref[...], other_ref[...]
    cross = jnp.concatenate([jnp.where(first, kept, other), jnp.where(first, other, kept)], 0)
    projected = mm(w_ref[...], cross)
    y_ref[...] = projected
    solved = mm(w_ref[...], projected, ((0,), (0,)))
    r_ref[...] = t_ref[...] - mm(p_ref[...], solved)


def finish(inverse, kept, other, panel_group, trailing):
    vmem = pl.BlockSpec(memory_space=pltpu.VMEM)
    return pl.pallas_call(
        finish_kernel,
        out_shape=(
            jax.ShapeDtypeStruct((N, trailing.shape[1]), F32),
            jax.ShapeDtypeStruct(trailing.shape, F32),
        ),
        in_specs=[vmem] * 5,
        out_specs=(vmem, vmem),
        compiler_params=pltpu.CompilerParams(vmem_limit_bytes=32 * 2**20),
        name="finish",
    )(inverse, kept, other, panel_group, trailing)


def on_device(panel_block, trailing):
    along_x = [[z * X + x for x in range(X)] for z in range(Z)]
    along_z = [[z * X + x for z in range(Z)] for x in range(X)]
    half = lax.axis_index("half")
    rows = sent_to_all(panel_block, "dev", along_x).reshape(-1, N)
    panel_group = lax.all_gather(rows, "dev", axis=0, axis_index_groups=along_z, tiled=True)

    own = gram_shares(rows)
    share = lax.all_to_all(own, "dev", 0, 0, axis_index_groups=along_z, tiled=True).sum(0)
    share = share + swapped(share)
    share = sent_to_all(share, "grp").sum(0)
    shares = sent_to_all(share, "dev")
    panel_group, _ = lax.optimization_barrier((panel_group, share))

    cross = mm(panel_group, trailing, ((0,), (0,))).reshape(2, N // 2, -1)
    kept = lax.dynamic_index_in_dim(cross, half, 0, keepdims=False)
    given = lax.dynamic_index_in_dim(cross, 1 - half, 0, keepdims=False)
    kept = kept + swapped(given)
    shares, kept = lax.optimization_barrier((shares, kept))
    triangle, inverse, end = factor(shares)
    kept = sent_to_all(kept, "grp").sum(0)
    kept, _ = lax.optimization_barrier((kept, end))
    other = swapped(kept)
    projected, remainder = finish(inverse, kept, other, panel_group, trailing)
    return (triangle, projected, remainder)


def solution(mesh):
    placed = (P(("half", "grp", "dev"), None), P(("half", "grp"), "dev"))
    return jax.shard_map(
        on_device,
        mesh=mesh,
        in_specs=placed,
        out_specs=(P(), P(None, "dev"), P(("half", "grp"), "dev")),
        check_vma=False,
    )
```

```python
import jax
import jax.numpy as jnp
from jax import lax
from jax.experimental import pallas as pl
from jax.experimental.pallas import tpu as pltpu
from jax.sharding import PartitionSpec as P

N = 512
B = 128
V = 8
NB = N // B
NP = B // V
X = 4
Z = 8
ROWS = 32
SHARE_ROWS = B // Z
HI = lax.Precision.HIGHEST
F32 = jnp.float32


def across_lanes(v, c):
    return jnp.broadcast_to(v[:, c : c + 1], (V, B))


def across_rows(v, j):
    return jnp.broadcast_to(v[j : j + 1, :], (V, B))


def factor_block(m):
    row = lax.broadcasted_iota(jnp.int32, (V, B), 0)
    lane = lax.broadcasted_iota(jnp.int32, (V, B), 1)
    ups, invs = [], []
    for p in range(NP):
        r0 = p * V
        mp = m[p]
        diag = (lane >= r0) & (lane < r0 + V)
        eye = (lane == row + r0).astype(F32)
        b = [across_lanes(mp, r0 + j) for j in range(V)]
        low, low_e, full = mp, eye, jnp.where(diag, eye, mp)
        dv = jnp.ones((V, B), F32)
        for j in range(V):
            d = across_rows(b[j], j)
            dv = jnp.where(row == j, d, dv)
            mult = b[j] * (1.0 / d)
            mfull = jnp.where(row == j, 0.0, mult)
            mlow = jnp.where(row > j, mult, 0.0)
            for k in range(j + 1, V):
                b[k] = b[k] - mfull * across_rows(b[k], j)
            low = low - mlow * across_rows(low, j)
            low_e = low_e - mlow * across_rows(low_e, j)
            full = full - mfull * across_rows(full, j)
        rs = lax.rsqrt(dv)
        full = full * (1.0 / dv)
        ups.append(jnp.where(lane >= row + r0, low * rs, 0.0))
        invs.append(jnp.where(lane <= row + r0, jnp.where(diag, low_e, low) * rs, 0.0))
        if p + 1 < NP:
            f = [across_rows(full, j) for j in range(V)]
            for q in range(p + 1, NP):
                old = m[q]
                t = [across_lanes(old, r0 + j) * f[j] for j in range(V)]
                s = ((t[0] + t[1]) + (t[2] + t[3])) + ((t[4] + t[5]) + (t[6] + t[7]))
                m[q] = jnp.where(diag, 0.0, old) - s
    return jnp.concatenate(ups, 0), jnp.concatenate(invs, 0)


def mm(a, b, dims=((1,), (0,))):
    return lax.dot_general(a, b, (dims, ((), ())), precision=HI, preferred_element_type=F32)


def tile(g_ref, block, t):
    s = block * SHARE_ROWS + (t % 2) * V
    return g_ref[t // 2 * X + s // 40, s % 40 : s % 40 + V, :]


def factor_kernel(g_ref, r_ref, w_ref, m_ref):
    block = 0
    for i in range(NB):
        for j in range(i, NB):
            for t in range(NP):
                m_ref[i * B + V * t : i * B + V * (t + 1), j * B : (j + 1) * B] = tile(g_ref, block, t)
            block += 1
    r_ref[...] = jnp.zeros_like(r_ref)
    for k in range(NB):
        o = k * B
        e = o + B
        u, v = factor_block([m_ref[o + V * i : o + V * (i + 1), o:e] for i in range(NP)])
        r_ref[o:e, o:e] = u
        w_ref[o:e, o:e] = v
        if k:
            w_ref[o:e, :o] = mm(v, m_ref[o:e, :o])
        if k + 1 < NB:
            w_ref[o:e, e:] = jnp.zeros((B, N - e), F32)
            ps = mm(v, m_ref[o:e, e:])
            r_ref[o:e, e:] = ps
            for i in range(k + 1, NB):
                q, lt = i * B, ps[:, (i - k - 1) * B : (i - k) * B].T
                m_ref[q : q + B, q:] = m_ref[q : q + B, q:] - mm(lt, ps[:, q - e :])
                if k:
                    m_ref[q : q + B, :o] = m_ref[q : q + B, :o] - mm(lt, w_ref[o:e, :o])
                m_ref[q : q + B, o:e] = -mm(lt, v)


def factor(shares):
    out = jax.ShapeDtypeStruct((N, N), F32)
    vmem = pl.BlockSpec(memory_space=pltpu.VMEM)
    return pl.pallas_call(
        factor_kernel,
        out_shape=(out, out),
        scratch_shapes=[pltpu.VMEM((N, N), F32)],
        in_specs=[vmem],
        out_specs=(vmem, vmem),
        compiler_params=pltpu.CompilerParams(vmem_limit_bytes=32 * 2**20),
        cost_estimate=pl.CostEstimate(flops=20_000_000_000, bytes_accessed=3 * 2**20, transcendentals=0),
        name="factor",
    )(shares)


def sent_to_all(x, axis, groups=None):
    size = len(groups[0]) if groups else lax.axis_size(axis)
    copies = jnp.broadcast_to(x[None], (size, *x.shape))
    return lax.all_to_all(copies, axis, 0, 0, axis_index_groups=groups, tiled=True)


def swapped(x):
    return lax.ppermute(x, "half", [(0, 1), (1, 0)])


VMEM = pl.BlockSpec(memory_space=pltpu.VMEM)
PARAMS = pltpu.CompilerParams(vmem_limit_bytes=32 * 2**20)


def gram_kernel(p_ref, own_ref, t_ref):
    first = lax.axis_index("dev") // X * SHARE_ROWS
    for i in range(NB):
        t_ref[i * B : (i + 1) * B, :] = p_ref[:, i * B : (i + 1) * B].T
    left = jnp.concatenate([t_ref[pl.ds(pl.multiple_of(i * B + first, SHARE_ROWS), SHARE_ROWS), :] for i in range(NB)], 0)
    g = mm(left, p_ref[...])
    block = 0
    for i in range(NB):
        for j in range(i, NB):
            for t in range(SHARE_ROWS // V):
                s, row = block * SHARE_ROWS + t * V, i * SHARE_ROWS + t * V
                own_ref[s // 40, s % 40 : s % 40 + V, :] = g[row : row + V, j * B : (j + 1) * B]
            block += 1


def gram_shares(rows):
    return pl.pallas_call(
        gram_kernel,
        out_shape=jax.ShapeDtypeStruct((X, 40, B), F32),
        scratch_shapes=[pltpu.VMEM((N, rows.shape[0]), F32)],
        in_specs=[VMEM],
        out_specs=VMEM,
        compiler_params=PARAMS,
        name="gram",
    )(rows)


def slab_rows(k, z):
    x = (lax.axis_index("dev") + (X - k)) % X
    return pl.ds(pl.multiple_of((z * X + x) * ROWS, ROWS), ROWS)


def cross_kernel(p0, p1, p2, p3, t_ref, kept_ref, given_ref):
    total = None
    for k, p_ref in enumerate((p0, p1, p2, p3)):
        t = jnp.concatenate([t_ref[slab_rows(k, z), :] for z in range(Z)], 0)
        part = mm(t.T, p_ref[...])
        total = part if total is None else total + part
    first = lax.axis_index("half") == 0
    low, high = total[:, : N // 2], total[:, N // 2 :]
    kept_ref[...] = jnp.where(first, low, high)
    given_ref[...] = jnp.where(first, high, low)


def cross_halves(blocks, trailing):
    out = jax.ShapeDtypeStruct((trailing.shape[1], N // 2), F32)
    return pl.pallas_call(
        cross_kernel,
        out_shape=(out, out),
        in_specs=[VMEM] * 5,
        out_specs=(VMEM, VMEM),
        compiler_params=PARAMS,
        cost_estimate=pl.CostEstimate(flops=2_000_000_000, bytes_accessed=3 * 2**20, transcendentals=0),
        name="cross",
    )(*blocks, trailing)


def finish_kernel(w_ref, kept_ref, other_ref, p0, p1, p2, p3, t_ref, y_ref, r_ref):
    first = lax.axis_index("half") == 0
    kept, other = kept_ref[...], other_ref[...]
    cross = jnp.concatenate([jnp.where(first, kept, other), jnp.where(first, other, kept)], 1)
    projected = mm(cross, w_ref[...], ((1,), (1,)))
    y_ref[...] = projected.T
    solved = mm(projected, w_ref[...])
    for k, p_ref in enumerate((p0, p1, p2, p3)):
        part = mm(p_ref[...], solved, ((1,), (1,)))
        for z in range(Z):
            here = slab_rows(k, z)
            r_ref[here, :] = t_ref[here, :] - part[z * ROWS : (z + 1) * ROWS, :]


def finish(inverse, kept, other, blocks, trailing):
    return pl.pallas_call(
        finish_kernel,
        out_shape=(
            jax.ShapeDtypeStruct((N, trailing.shape[1]), F32),
            jax.ShapeDtypeStruct(trailing.shape, F32),
        ),
        in_specs=[VMEM] * 8,
        out_specs=(VMEM, VMEM),
        compiler_params=PARAMS,
        name="finish",
    )(inverse, kept, other, *blocks, trailing)


def on_device(panel_block, trailing):
    along_x = [[z * X + x for x in range(X)] for z in range(Z)]
    along_z = [[z * X + x for z in range(Z)] for x in range(X)]
    rows = sent_to_all(panel_block, "dev", along_z).reshape(-1, N)

    own = gram_shares(rows)
    share = lax.all_to_all(own, "dev", 0, 0, axis_index_groups=along_x, tiled=True).sum(0)
    rows, _ = lax.optimization_barrier((rows, own))
    blocks = [rows]
    for k in range(1, X):
        moves = [(z * X + x, z * X + (x + k) % X) for z in range(Z) for x in range(X)]
        blocks.append(lax.ppermute(rows, "dev", moves))
    share = share + swapped(share)
    share = sent_to_all(share, "grp").sum(0)
    shares = sent_to_all(share, "dev")

    kept, given = cross_halves(blocks, trailing)
    kept = kept + swapped(given)
    groups = lax.axis_size("grp")
    kept, _ = lax.optimization_barrier((kept, share))
    parts = [lax.ppermute(kept, "grp", [(g, (g + k) % groups) for g in range(groups)]) for k in (4, 3, 5, 2, 6, 1, 7)]
    kept = sum(parts, kept)
    other = swapped(kept)

    triangle, inverse = factor(shares)
    projected, remainder = finish(inverse, kept, other, blocks, trailing)
    return (triangle, projected, remainder)


def solution(mesh):
    placed = (P(("half", "grp", "dev"), None), P(("half", "grp"), "dev"))
    return jax.shard_map(
        on_device,
        mesh=mesh,
        in_specs=placed,
        out_specs=(P(), P(None, "dev"), P(("half", "grp"), "dev")),
        check_vma=False,
    )
```

```python
import jax
import jax.numpy as jnp
from jax import lax
from jax.experimental import pallas as pl
from jax.experimental.pallas import tpu as pltpu
from jax.sharding import PartitionSpec as P

N = 512
B = 128
V = 8
NB = N // B
NP = B // V
X = 4
Z = 8
PARTS = 4
SHARE_ROWS = B // X
HI = lax.Precision.HIGHEST
F32 = jnp.float32


def across_lanes(v, c):
    return jnp.broadcast_to(v[:, c : c + 1], (V, B))


def across_rows(v, j):
    return jnp.broadcast_to(v[j : j + 1, :], (V, B))


def factor_block(m):
    row = lax.broadcasted_iota(jnp.int32, (V, B), 0)
    lane = lax.broadcasted_iota(jnp.int32, (V, B), 1)
    ups, invs = [], []
    for p in range(NP):
        r0 = p * V
        mp = m[p]
        diag = (lane >= r0) & (lane < r0 + V)
        eye = (lane == row + r0).astype(F32)
        b = [across_lanes(mp, r0 + j) for j in range(V)]
        low, low_e, full = mp, eye, jnp.where(diag, eye, mp)
        dv = jnp.ones((V, B), F32)
        for j in range(V):
            d = across_rows(b[j], j)
            dv = jnp.where(row == j, d, dv)
            mult = b[j] * (1.0 / d)
            mfull = jnp.where(row == j, 0.0, mult)
            mlow = jnp.where(row > j, mult, 0.0)
            for k in range(j + 1, V):
                b[k] = b[k] - mfull * across_rows(b[k], j)
            low = low - mlow * across_rows(low, j)
            low_e = low_e - mlow * across_rows(low_e, j)
            full = full - mfull * across_rows(full, j)
        rs = lax.rsqrt(dv)
        full = full * (1.0 / dv)
        ups.append(jnp.where(lane >= row + r0, low * rs, 0.0))
        invs.append(jnp.where(lane <= row + r0, jnp.where(diag, low_e, low) * rs, 0.0))
        if p + 1 < NP:
            f = [across_rows(full, j) for j in range(V)]
            for q in range(p + 1, NP):
                old = m[q]
                t = [across_lanes(old, r0 + j) * f[j] for j in range(V)]
                s = ((t[0] + t[1]) + (t[2] + t[3])) + ((t[4] + t[5]) + (t[6] + t[7]))
                m[q] = jnp.where(diag, 0.0, old) - s
    return jnp.concatenate(ups, 0), jnp.concatenate(invs, 0)


def mm(a, b, dims=((1,), (0,))):
    return lax.dot_general(a, b, (dims, ((), ())), precision=HI, preferred_element_type=F32)


def tile(g_ref, block, t):
    s = block * SHARE_ROWS + (t % 4) * V
    return g_ref[s // 40 * X + t // 4, s % 40 : s % 40 + V, :]


def factor_kernel(g_ref, after_ref, r_ref, w_ref, end_ref, m_ref):
    block = 0
    for i in range(NB):
        for j in range(i, NB):
            for t in range(NP):
                m_ref[i * B + V * t : i * B + V * (t + 1), j * B : (j + 1) * B] = tile(g_ref, block, t)
            block += 1
    r_ref[...] = jnp.zeros_like(r_ref)
    for k in range(NB):
        o = k * B
        e = o + B
        u, v = factor_block([m_ref[o + V * i : o + V * (i + 1), o:e] for i in range(NP)])
        r_ref[o:e, o:e] = u
        w_ref[o:e, o:e] = v
        if k:
            w_ref[o:e, :o] = mm(v, m_ref[o:e, :o])
        if k + 1 < NB:
            w_ref[o:e, e:] = jnp.zeros((B, N - e), F32)
            ps = mm(v, m_ref[o:e, e:])
            r_ref[o:e, e:] = ps
            for i in range(k + 1, NB):
                q, lt = i * B, ps[:, (i - k - 1) * B : (i - k) * B].T
                m_ref[q : q + B, q:] = m_ref[q : q + B, q:] - mm(lt, ps[:, q - e :])
                if k:
                    m_ref[q : q + B, :o] = m_ref[q : q + B, :o] - mm(lt, w_ref[o:e, :o])
                m_ref[q : q + B, o:e] = -mm(lt, v)
    end_ref[...] = jnp.zeros_like(end_ref)


def factor(shares, after):
    out = jax.ShapeDtypeStruct((N, N), F32)
    vmem = pl.BlockSpec(memory_space=pltpu.VMEM)
    return pl.pallas_call(
        factor_kernel,
        out_shape=(out, out, jax.ShapeDtypeStruct((V, B), F32)),
        scratch_shapes=[pltpu.VMEM((N, N), F32)],
        in_specs=[vmem, pl.BlockSpec(memory_space=pl.ANY)],
        out_specs=(vmem, vmem, vmem),
        compiler_params=pltpu.CompilerParams(vmem_limit_bytes=16 * 2**20),
        cost_estimate=pl.CostEstimate(flops=20_000_000_000, bytes_accessed=3 * 2**20, transcendentals=0),
        name="factor",
    )(shares, after)


def sent_to_all(x, axis, groups=None):
    size = len(groups[0]) if groups else lax.axis_size(axis)
    copies = jnp.broadcast_to(x[None], (size, *x.shape))
    return lax.all_to_all(copies, axis, 0, 0, axis_index_groups=groups, tiled=True)


def swapped(x):
    return lax.ppermute(x, "half", [(0, 1), (1, 0)])


VMEM = pl.BlockSpec(memory_space=pltpu.VMEM)
PARAMS = pltpu.CompilerParams(vmem_limit_bytes=16 * 2**20)


def gram_kernel(p_ref, own_ref, t_ref):
    first = lax.axis_index("dev") % X * SHARE_ROWS
    for i in range(NB):
        t_ref[i * B : (i + 1) * B, :] = p_ref[:, i * B : (i + 1) * B].T
    left = jnp.concatenate([t_ref[pl.ds(pl.multiple_of(i * B + first, SHARE_ROWS), SHARE_ROWS), :] for i in range(NB)], 0)
    g = mm(left, p_ref[...])
    block = 0
    for i in range(NB):
        for j in range(i, NB):
            for t in range(SHARE_ROWS // V):
                s, row = block * SHARE_ROWS + t * V, i * SHARE_ROWS + t * V
                own_ref[s // 40, s % 40 : s % 40 + V, :] = g[row : row + V, j * B : (j + 1) * B]
            block += 1


def gram_shares(rows):
    return pl.pallas_call(
        gram_kernel,
        out_shape=jax.ShapeDtypeStruct((Z, 40, B), F32),
        scratch_shapes=[pltpu.VMEM((N, rows.shape[0]), F32)],
        in_specs=[VMEM],
        out_specs=VMEM,
        compiler_params=PARAMS,
        name="gram",
    )(rows)


def cross_kernel(p_ref, t_ref, kept_ref, given_ref):
    rows = p_ref.shape[0] // PARTS
    total = None
    for i in range(PARTS):
        here = slice(i * rows, (i + 1) * rows)
        part = mm(t_ref[here, :].T, p_ref[here, :])
        total = part if total is None else total + part
    first = lax.axis_index("half") == 0
    low, high = total[:, : N // 2], total[:, N // 2 :]
    kept_ref[...] = jnp.where(first, low, high)
    given_ref[...] = jnp.where(first, high, low)


def cross_halves(panel_group, trailing):
    out = jax.ShapeDtypeStruct((trailing.shape[1], N // 2), F32)
    return pl.pallas_call(
        cross_kernel,
        out_shape=(out, out),
        in_specs=[VMEM] * 2,
        out_specs=(VMEM, VMEM),
        compiler_params=PARAMS,
        cost_estimate=pl.CostEstimate(flops=2_000_000_000, bytes_accessed=3 * 2**20, transcendentals=0),
        name="cross",
    )(panel_group, trailing)


def finish_kernel(w_ref, kept_ref, other_ref, p_ref, t_ref, end_ref, y_ref, r_ref):
    first = lax.axis_index("half") == 0
    kept, other = kept_ref[...], other_ref[...]
    cross = jnp.concatenate([jnp.where(first, kept, other), jnp.where(first, other, kept)], 1)
    projected = mm(cross, w_ref[...], ((1,), (1,)))
    y_ref[...] = projected.T
    solved = mm(projected, w_ref[...])
    r_ref[...] = t_ref[...] - mm(p_ref[...], solved, ((1,), (1,)))


def finish(inverse, kept, other, panel_group, trailing, end):
    return pl.pallas_call(
        finish_kernel,
        out_shape=(
            jax.ShapeDtypeStruct((N, trailing.shape[1]), F32),
            jax.ShapeDtypeStruct(trailing.shape, F32),
        ),
        in_specs=[VMEM] * 6,
        out_specs=(VMEM, VMEM),
        compiler_params=PARAMS,
        name="finish",
    )(inverse, kept, other, panel_group, trailing, end)


def on_device(panel_block, trailing):
    along_x = [[z * X + x for x in range(X)] for z in range(Z)]
    along_z = [[z * X + x for z in range(Z)] for x in range(X)]
    groups = lax.axis_size("grp")
    alternate = [list(range(first, groups, 2)) for first in range(2)]
    rows = sent_to_all(panel_block, "dev", along_x).reshape(-1, N)
    panel_group = lax.all_gather(rows, "dev", axis=0, axis_index_groups=along_z, tiled=True)

    own = gram_shares(rows)
    share = lax.all_to_all(own, "dev", 0, 0, axis_index_groups=along_z, tiled=True).sum(0)
    share = share + swapped(share)
    share = sent_to_all(share, "grp").sum(0)
    shares = sent_to_all(share, "dev")

    panel_group, _ = lax.optimization_barrier((panel_group, share))
    kept, given = cross_halves(panel_group, trailing)
    kept = kept + swapped(given)
    kept = kept + lax.ppermute(kept, "grp", [(g, g ^ 1) for g in range(groups)])

    triangle, inverse, end = factor(shares, kept)
    kept = sent_to_all(kept, "grp", alternate).sum(0)
    kept, end = lax.optimization_barrier((kept, end))
    other = swapped(kept)
    projected, remainder = finish(inverse, kept, other, panel_group, trailing, end)
    return (triangle, projected, remainder)


def solution(mesh):
    placed = (P(("half", "grp", "dev"), None), P(("half", "grp"), "dev"))
    return jax.shard_map(
        on_device,
        mesh=mesh,
        in_specs=placed,
        out_specs=(P(), P(None, "dev"), P(("half", "grp"), "dev")),
        check_vma=False,
    )
```

```python
import jax
import jax.numpy as jnp
from jax import lax
from jax.experimental import pallas as pl
from jax.experimental.pallas import tpu as pltpu
from jax.sharding import PartitionSpec as P

N = 512
B = 128
V = 8
NB = N // B
NP = B // V
X = 4
Z = 8
PARTS = 4
GROUP = 4
SHARE_ROWS = B // X
HI = lax.Precision.HIGHEST
F32 = jnp.float32
BF16 = jnp.bfloat16
VMEM = pl.BlockSpec(memory_space=pltpu.VMEM)
PARAMS = pltpu.CompilerParams(vmem_limit_bytes=16 * 2**20)


def mm(a, b, dims=((1,), (0,))):
    return lax.dot_general(a, b, (dims, ((), ())), precision=HI, preferred_element_type=F32)


def three(x):
    high = x.astype(BF16)
    rest = x - high.astype(F32)
    middle = rest.astype(BF16)
    return high, middle, (rest - middle.astype(F32)).astype(BF16)


def left(x, axis):
    h, m, l = three(x)
    return jnp.concatenate([h, h, m, m, h, l], axis)


def right(x, axis):
    h, m, l = three(x)
    return jnp.concatenate([h, m, h, m, l, h], axis)


def dot(a, b, dims):
    return lax.dot_general(a, b, (dims, ((), ())), preferred_element_type=F32)


def across_lanes(v, c):
    return jnp.broadcast_to(v[:, c : c + 1], (V, B))


def across_rows(v, j):
    return jnp.broadcast_to(v[j : j + 1, :], (V, B))


def eliminated(x, m0, m1, j, keep):
    return jnp.where(keep, x, 0.0) - m0 * across_rows(x, j) - m1 * across_rows(x, j + 1)


def total(terms):
    while len(terms) > 1:
        terms = [terms[i] + terms[i + 1] for i in range(0, len(terms), 2)]
    return terms[0]


def factor_block(m):
    row = lax.broadcasted_iota(jnp.int32, (V, B), 0)
    lane = lax.broadcasted_iota(jnp.int32, (V, B), 1)
    ups, invs, b = [], [], None
    for p in range(NP):
        r0 = p * V
        mp = m[p]
        diag = (lane >= r0) & (lane < r0 + V)
        eye = (lane == row + r0).astype(F32)
        more = p + 1 < NP
        if b is None:
            b = [across_lanes(mp, r0 + j) for j in range(V)]
        ahead = [across_lanes(mp, r0 + V + j) for j in range(V)] if more else []
        low, low_e, full = mp, eye, jnp.where(diag, eye, mp)
        dv = jnp.ones((V, B), F32)
        for j in range(0, V, 2):
            d, x, c = across_rows(b[j], j), across_rows(b[j], j + 1), across_rows(b[j + 1], j + 1)
            det = d * c - x * x
            over_det, over_d = 1.0 / det, 1.0 / d
            u0, u1 = b[j] * c - b[j + 1] * x, b[j + 1] * d - b[j] * x
            first, second, below = row == j, row == j + 1, row > j + 1
            keep = ~(first | second)
            m0 = jnp.where(first, -c, jnp.where(second, x, u0)) * over_det
            m1 = jnp.where(first, x, jnp.where(second, -d, u1)) * over_det
            for k in range(j + 2, V):
                b[k] = eliminated(b[k], m0, m1, j, keep)
            ahead = [eliminated(n, m0, m1, j, keep) for n in ahead]
            l0 = jnp.where(below, m0, jnp.where(second, x * over_d, 0.0))
            l1 = jnp.where(below, m1, 0.0)
            low = low - l0 * across_rows(low, j) - l1 * across_rows(low, j + 1)
            low_e = low_e - l0 * across_rows(low_e, j) - l1 * across_rows(low_e, j + 1)
            full = eliminated(full, m0, m1, j, keep)
            dv = jnp.where(first, d, jnp.where(second, det * over_d, dv))
        rs = lax.rsqrt(dv)
        ups.append(jnp.where(lane >= row + r0, low * rs, 0.0))
        invs.append(jnp.where(lane <= row + r0, jnp.where(diag, low_e, low) * rs, 0.0))
        if not more:
            break
        end = (p // GROUP + 1) * GROUP
        here = [across_lanes(m[p + 1], r0 + j) for j in range(V)]
        b = [
            across_lanes(m[p + 1], r0 + V + k) - total([here[j] * across_rows(ahead[k], j) for j in range(V)])
            for k in range(V)
        ]
        f = [across_rows(full, j) for j in range(V)]
        for q in range(p + 1, min(end + 1, NP)):
            old = m[q]
            m[q] = jnp.where(diag, 0.0, old) - total([across_lanes(old, r0 + j) * f[j] for j in range(V)])
        if p + 1 == end and end + 1 < NP:
            u, w = jnp.concatenate(ups[-GROUP:], 0), jnp.concatenate(invs[-GROUP:], 0)
            inverse_lanes = lax.broadcasted_iota(jnp.int32, u.shape, 1) < end * V
            update = dot(left(u, 0), right(jnp.where(inverse_lanes, w, u), 0), ((0,), (0,)))
            done = (lane >= (end - GROUP) * V) & (lane < end * V)
            for q in range(end + 1, NP):
                m[q] = jnp.where(done, 0.0, m[q]) - update[q * V : (q + 1) * V, :]
    return jnp.concatenate(ups, 0), jnp.concatenate(invs, 0)


def tile(g_ref, block, t):
    s = block * SHARE_ROWS + t % 4 * V
    return g_ref[s // 40 * X + t // 4, s % 40 : s % 40 + V, :]


def factor_kernel(g_ref, after_ref, r_ref, w_ref, end_ref, m_ref):
    block = 0
    for i in range(NB):
        for j in range(i, NB):
            for t in range(NP):
                m_ref[i * B + V * t : i * B + V * (t + 1), j * B : (j + 1) * B] = tile(g_ref, block, t)
            block += 1
    for k in range(NB):
        o = k * B
        e = o + B
        f = e + B
        u, v = factor_block([m_ref[o + V * i : o + V * (i + 1), o:e] for i in range(NP)])
        v_left = left(v, 1)
        r_ref[o:e, o:e] = u
        w_ref[o:e, o:e] = v
        if e < N:
            ps = dot(v_left, right(m_ref[o:e, e:], 0), ((1,), (0,)))
            r_ref[o:e, e:] = ps
            w_ref[o:e, e:] = jnp.zeros((B, N - e), F32)
            p_left, p_right = left(ps, 0), right(ps, 0)
            m_ref[e:f, e:] = m_ref[e:f, e:] - dot(p_left[:, :B], p_right, ((0,), (0,)))
            if f < N:
                m_ref[f:, f:] = m_ref[f:, f:] - dot(p_left[:, B:], p_right[:, B:], ((0,), (0,)))
        if k:
            wl = dot(v_left, right(m_ref[o:e, :o], 0), ((1,), (0,)))
            w_ref[o:e, :o] = wl
            r_ref[o:e, :o] = jnp.zeros((B, o), F32)
        if e < N:
            if k:
                m_ref[e:, :o] = m_ref[e:, :o] - dot(p_left, right(wl, 0), ((0,), (0,)))
            m_ref[e:, o:e] = -dot(p_left, right(v, 0), ((0,), (0,)))
    end_ref[...] = jnp.zeros_like(end_ref)


def factor(shares, after):
    out = jax.ShapeDtypeStruct((N, N), F32)
    return pl.pallas_call(
        factor_kernel,
        out_shape=(out, out, jax.ShapeDtypeStruct((V, B), F32)),
        scratch_shapes=[pltpu.VMEM((N, N), F32)],
        in_specs=[VMEM, pl.BlockSpec(memory_space=pl.ANY)],
        out_specs=(VMEM, VMEM, VMEM),
        compiler_params=PARAMS,
        cost_estimate=pl.CostEstimate(flops=20_000_000_000, bytes_accessed=3 * 2**20, transcendentals=0),
        name="factor",
    )(shares, after)


def sent_to_all(x, axis, groups=None):
    size = len(groups[0]) if groups else lax.axis_size(axis)
    copies = jnp.broadcast_to(x[None], (size, *x.shape))
    return lax.all_to_all(copies, axis, 0, 0, axis_index_groups=groups, tiled=True)


def swapped(x):
    return lax.ppermute(x, "half", [(0, 1), (1, 0)])


def gram_kernel(p_ref, own_ref, t_ref):
    first = lax.axis_index("dev") % X * SHARE_ROWS
    for i in range(NB):
        t_ref[i * B : (i + 1) * B, :] = p_ref[:, i * B : (i + 1) * B].T
    left = jnp.concatenate([t_ref[pl.ds(pl.multiple_of(i * B + first, SHARE_ROWS), SHARE_ROWS), :] for i in range(NB)], 0)
    g = mm(left, p_ref[...])
    block = 0
    for i in range(NB):
        for j in range(i, NB):
            for t in range(SHARE_ROWS // V):
                s, row = block * SHARE_ROWS + t * V, i * SHARE_ROWS + t * V
                own_ref[s // 40, s % 40 : s % 40 + V, :] = g[row : row + V, j * B : (j + 1) * B]
            block += 1


def gram_shares(rows):
    return pl.pallas_call(
        gram_kernel,
        out_shape=jax.ShapeDtypeStruct((Z, 40, B), F32),
        scratch_shapes=[pltpu.VMEM((N, rows.shape[0]), F32)],
        in_specs=[VMEM],
        out_specs=VMEM,
        compiler_params=PARAMS,
        name="gram",
    )(rows)


def cross_kernel(p_ref, t_ref, kept_ref, given_ref):
    rows = p_ref.shape[0] // PARTS
    product = None
    for i in range(PARTS):
        here = slice(i * rows, (i + 1) * rows)
        part = mm(t_ref[here, :].T, p_ref[here, :])
        product = part if product is None else product + part
    first = lax.axis_index("half") == 0
    low, high = product[:, : N // 2], product[:, N // 2 :]
    kept_ref[...] = jnp.where(first, low, high)
    given_ref[...] = jnp.where(first, high, low)


def cross_halves(panel_group, trailing):
    out = jax.ShapeDtypeStruct((trailing.shape[1], N // 2), F32)
    return pl.pallas_call(
        cross_kernel,
        out_shape=(out, out),
        in_specs=[VMEM] * 2,
        out_specs=(VMEM,) * 2,
        compiler_params=PARAMS,
        cost_estimate=pl.CostEstimate(flops=2_000_000_000, bytes_accessed=3 * 2**20, transcendentals=0),
        name="cross",
    )(panel_group, trailing)


def finish_kernel(w_ref, kept_ref, other_ref, p_ref, t_ref, end_ref, y_ref, r_ref):
    first = lax.axis_index("half") == 0
    kept, other = kept_ref[...], other_ref[...]
    cross = jnp.concatenate([jnp.where(first, kept, other), jnp.where(first, other, kept)], 1)
    projected = mm(cross, w_ref[...], ((1,), (1,)))
    y_ref[...] = projected.T
    solved = mm(projected, w_ref[...])
    r_ref[...] = t_ref[...] - mm(p_ref[...], solved, ((1,), (1,)))


def finish(inverse, kept, other, panel_group, trailing, end):
    return pl.pallas_call(
        finish_kernel,
        out_shape=(
            jax.ShapeDtypeStruct((N, trailing.shape[1]), F32),
            jax.ShapeDtypeStruct(trailing.shape, F32),
        ),
        in_specs=[VMEM] * 6,
        out_specs=(VMEM, VMEM),
        compiler_params=PARAMS,
        name="finish",
    )(inverse, kept, other, panel_group, trailing, end)


def on_device(panel_block, trailing):
    along_x = [[z * X + x for x in range(X)] for z in range(Z)]
    along_z = [[z * X + x for z in range(Z)] for x in range(X)]
    groups = lax.axis_size("grp")
    alternate = [list(range(first, groups, 2)) for first in range(2)]
    rows = sent_to_all(panel_block, "dev", along_x).reshape(-1, N)
    panel_group = lax.all_gather(rows, "dev", axis=0, axis_index_groups=along_z, tiled=True)

    own = gram_shares(rows)
    share = lax.all_to_all(own, "dev", 0, 0, axis_index_groups=along_z, tiled=True).sum(0)
    share = share + swapped(share)
    share = sent_to_all(share, "grp").sum(0)
    shares = sent_to_all(share, "dev")

    panel_group, _ = lax.optimization_barrier((panel_group, share))
    kept, given = cross_halves(panel_group, trailing)
    kept = kept + swapped(given)
    kept = kept + lax.ppermute(kept, "grp", [(g, g ^ 1) for g in range(groups)])

    triangle, inverse, end = factor(shares, kept)
    kept = sent_to_all(kept, "grp", alternate).sum(0)
    kept, end = lax.optimization_barrier((kept, end))
    other = swapped(kept)
    projected, remainder = finish(inverse, kept, other, panel_group, trailing, end)
    return (triangle, projected, remainder)


def solution(mesh):
    placed = (P(("half", "grp", "dev"), None), P(("half", "grp"), "dev"))
    return jax.shard_map(
        on_device,
        mesh=mesh,
        in_specs=placed,
        out_specs=(P(), P(None, "dev"), P(("half", "grp"), "dev")),
        check_vma=False,
    )
```

```python
import jax
import jax.numpy as jnp
from jax import lax
from jax.experimental import pallas as pl
from jax.experimental.pallas import tpu as pltpu
from jax.sharding import PartitionSpec as P

N = 512
B = 128
V = 8
NB = N // B
NP = B // V
X = 4
Z = 8
ROWS = 32
GROUP = 4
SHARE_ROWS = B // Z
HI = lax.Precision.HIGHEST
F32 = jnp.float32
BF16 = jnp.bfloat16
VMEM = pl.BlockSpec(memory_space=pltpu.VMEM)
PARAMS = pltpu.CompilerParams(vmem_limit_bytes=16 * 2**20)


def mm(a, b, dims=((1,), (0,))):
    return lax.dot_general(a, b, (dims, ((), ())), precision=HI, preferred_element_type=F32)


def three(x):
    high = x.astype(BF16)
    rest = x - high.astype(F32)
    middle = rest.astype(BF16)
    return high, middle, (rest - middle.astype(F32)).astype(BF16)


def left(x, axis):
    h, m, l = three(x)
    return jnp.concatenate([h, h, m, m, h, l], axis)


def right(x, axis):
    h, m, l = three(x)
    return jnp.concatenate([h, m, h, m, l, h], axis)


def dot(a, b, dims):
    return lax.dot_general(a, b, (dims, ((), ())), preferred_element_type=F32)


def across_lanes(v, c):
    return jnp.broadcast_to(v[:, c : c + 1], (V, B))


def across_rows(v, j):
    return jnp.broadcast_to(v[j : j + 1, :], (V, B))


def eliminated(x, m0, m1, j, keep):
    return jnp.where(keep, x, 0.0) - m0 * across_rows(x, j) - m1 * across_rows(x, j + 1)


def total(terms):
    while len(terms) > 1:
        terms = [terms[i] + terms[i + 1] for i in range(0, len(terms), 2)]
    return terms[0]


def factor_block(m):
    row = lax.broadcasted_iota(jnp.int32, (V, B), 0)
    lane = lax.broadcasted_iota(jnp.int32, (V, B), 1)
    ups, invs, b = [], [], None
    for p in range(NP):
        r0 = p * V
        mp = m[p]
        diag = (lane >= r0) & (lane < r0 + V)
        eye = (lane == row + r0).astype(F32)
        more = p + 1 < NP
        if b is None:
            b = [across_lanes(mp, r0 + j) for j in range(V)]
        ahead = [across_lanes(mp, r0 + V + j) for j in range(V)] if more else []
        low, low_e, full = mp, eye, jnp.where(diag, eye, mp)
        dv = jnp.ones((V, B), F32)
        for j in range(0, V, 2):
            d, x, c = across_rows(b[j], j), across_rows(b[j], j + 1), across_rows(b[j + 1], j + 1)
            det = d * c - x * x
            over_det, over_d = 1.0 / det, 1.0 / d
            u0, u1 = b[j] * c - b[j + 1] * x, b[j + 1] * d - b[j] * x
            first, second, below = row == j, row == j + 1, row > j + 1
            keep = ~(first | second)
            m0 = jnp.where(first, -c, jnp.where(second, x, u0)) * over_det
            m1 = jnp.where(first, x, jnp.where(second, -d, u1)) * over_det
            for k in range(j + 2, V):
                b[k] = eliminated(b[k], m0, m1, j, keep)
            ahead = [eliminated(n, m0, m1, j, keep) for n in ahead]
            l0 = jnp.where(below, m0, jnp.where(second, x * over_d, 0.0))
            l1 = jnp.where(below, m1, 0.0)
            low = low - l0 * across_rows(low, j) - l1 * across_rows(low, j + 1)
            low_e = low_e - l0 * across_rows(low_e, j) - l1 * across_rows(low_e, j + 1)
            full = eliminated(full, m0, m1, j, keep)
            dv = jnp.where(first, d, jnp.where(second, det * over_d, dv))
        rs = lax.rsqrt(dv)
        ups.append(jnp.where(lane >= row + r0, low * rs, 0.0))
        invs.append(jnp.where(lane <= row + r0, jnp.where(diag, low_e, low) * rs, 0.0))
        if not more:
            break
        end = (p // GROUP + 1) * GROUP
        here = [across_lanes(m[p + 1], r0 + j) for j in range(V)]
        b = [
            across_lanes(m[p + 1], r0 + V + k) - total([here[j] * across_rows(ahead[k], j) for j in range(V)])
            for k in range(V)
        ]
        f = [across_rows(full, j) for j in range(V)]
        for q in range(p + 1, min(end + 1, NP)):
            old = m[q]
            m[q] = jnp.where(diag, 0.0, old) - total([across_lanes(old, r0 + j) * f[j] for j in range(V)])
        if p + 1 == end and end + 1 < NP:
            u, w = jnp.concatenate(ups[-GROUP:], 0), jnp.concatenate(invs[-GROUP:], 0)
            inverse_lanes = lax.broadcasted_iota(jnp.int32, u.shape, 1) < end * V
            update = dot(left(u, 0), right(jnp.where(inverse_lanes, w, u), 0), ((0,), (0,)))
            done = (lane >= (end - GROUP) * V) & (lane < end * V)
            for q in range(end + 1, NP):
                m[q] = jnp.where(done, 0.0, m[q]) - update[q * V : (q + 1) * V, :]
    return jnp.concatenate(ups, 0), jnp.concatenate(invs, 0)


def tile(g_ref, block, t):
    s = block * SHARE_ROWS + t % 2 * V
    return g_ref[t // 2 * X + s // 40, s % 40 : s % 40 + V, :]


def factor_kernel(g_ref, after_ref, r_ref, w_ref, m_ref):
    block = 0
    for i in range(NB):
        for j in range(i, NB):
            for t in range(NP):
                m_ref[i * B + V * t : i * B + V * (t + 1), j * B : (j + 1) * B] = tile(g_ref, block, t)
            block += 1
    for k in range(NB):
        o = k * B
        e = o + B
        f = e + B
        u, v = factor_block([m_ref[o + V * i : o + V * (i + 1), o:e] for i in range(NP)])
        v_left = left(v, 1)
        r_ref[o:e, o:e] = u
        w_ref[o:e, o:e] = v
        if e < N:
            ps = dot(v_left, right(m_ref[o:e, e:], 0), ((1,), (0,)))
            r_ref[o:e, e:] = ps
            w_ref[o:e, e:] = jnp.zeros((B, N - e), F32)
            p_left, p_right = left(ps, 0), right(ps, 0)
            m_ref[e:f, e:] = m_ref[e:f, e:] - dot(p_left[:, :B], p_right, ((0,), (0,)))
            if f < N:
                m_ref[f:, f:] = m_ref[f:, f:] - dot(p_left[:, B:], p_right[:, B:], ((0,), (0,)))
        if k:
            wl = dot(v_left, right(m_ref[o:e, :o], 0), ((1,), (0,)))
            w_ref[o:e, :o] = wl
            r_ref[o:e, :o] = jnp.zeros((B, o), F32)
        if e < N:
            if k:
                m_ref[e:, :o] = m_ref[e:, :o] - dot(p_left, right(wl, 0), ((0,), (0,)))
            m_ref[e:, o:e] = -dot(p_left, right(v, 0), ((0,), (0,)))


def factor(shares, after):
    out = jax.ShapeDtypeStruct((N, N), F32)
    return pl.pallas_call(
        factor_kernel,
        out_shape=(out, out),
        scratch_shapes=[pltpu.VMEM((N, N), F32)],
        in_specs=[VMEM, pl.BlockSpec(memory_space=pl.ANY)],
        out_specs=(VMEM, VMEM),
        compiler_params=PARAMS,
        cost_estimate=pl.CostEstimate(flops=20_000_000_000, bytes_accessed=3 * 2**20, transcendentals=0),
        name="factor",
    )(shares, after)


def sent_to_all(x, axis, groups=None):
    size = len(groups[0]) if groups else lax.axis_size(axis)
    copies = jnp.broadcast_to(x[None], (size, *x.shape))
    return lax.all_to_all(copies, axis, 0, 0, axis_index_groups=groups, tiled=True)


def swapped(x):
    return lax.ppermute(x, "half", [(0, 1), (1, 0)])


def gram_kernel(p_ref, own_ref, t_ref):
    first = lax.axis_index("dev") // X * SHARE_ROWS
    for i in range(NB):
        t_ref[i * B : (i + 1) * B, :] = p_ref[:, i * B : (i + 1) * B].T
    left = jnp.concatenate([t_ref[pl.ds(pl.multiple_of(i * B + first, SHARE_ROWS), SHARE_ROWS), :] for i in range(NB)], 0)
    g = mm(left, p_ref[...])
    block = 0
    for i in range(NB):
        for j in range(i, NB):
            for t in range(SHARE_ROWS // V):
                s, row = block * SHARE_ROWS + t * V, i * SHARE_ROWS + t * V
                own_ref[s // 40, s % 40 : s % 40 + V, :] = g[row : row + V, j * B : (j + 1) * B]
            block += 1


def gram_shares(rows):
    return pl.pallas_call(
        gram_kernel,
        out_shape=jax.ShapeDtypeStruct((X, 40, B), F32),
        scratch_shapes=[pltpu.VMEM((N, rows.shape[0]), F32)],
        in_specs=[VMEM],
        out_specs=VMEM,
        compiler_params=PARAMS,
        name="gram",
    )(rows)


def slab_rows(k, z):
    x = (lax.axis_index("dev") + (X - k)) % X
    return pl.ds(pl.multiple_of((z * X + x) * ROWS, ROWS), ROWS)


def cross_kernel(p0, p1, p2, p3, t_ref, kept_ref, given_ref):
    product = None
    for k, p_ref in enumerate((p0, p1, p2, p3)):
        t = jnp.concatenate([t_ref[slab_rows(k, z), :] for z in range(Z)], 0)
        part = mm(t.T, p_ref[...])
        product = part if product is None else product + part
    first = lax.axis_index("half") == 0
    low, high = product[:, : N // 2], product[:, N // 2 :]
    kept_ref[...] = jnp.where(first, low, high)
    given_ref[...] = jnp.where(first, high, low)


def cross_halves(blocks, trailing):
    out = jax.ShapeDtypeStruct((trailing.shape[1], N // 2), F32)
    return pl.pallas_call(
        cross_kernel,
        out_shape=(out, out),
        in_specs=[VMEM] * 5,
        out_specs=(VMEM, VMEM),
        compiler_params=PARAMS,
        cost_estimate=pl.CostEstimate(flops=2_000_000_000, bytes_accessed=3 * 2**20, transcendentals=0),
        name="cross",
    )(*blocks, trailing)


def finish_kernel(w_ref, kept_ref, other_ref, p0, p1, p2, p3, t_ref, y_ref, r_ref):
    first = lax.axis_index("half") == 0
    kept, other = kept_ref[...], other_ref[...]
    cross = jnp.concatenate([jnp.where(first, kept, other), jnp.where(first, other, kept)], 1)
    projected = mm(cross, w_ref[...], ((1,), (1,)))
    y_ref[...] = projected.T
    solved = mm(projected, w_ref[...])
    for k, p_ref in enumerate((p0, p1, p2, p3)):
        part = mm(p_ref[...], solved, ((1,), (1,)))
        for z in range(Z):
            here = slab_rows(k, z)
            r_ref[here, :] = t_ref[here, :] - part[z * ROWS : (z + 1) * ROWS, :]


def finish(inverse, kept, other, blocks, trailing):
    return pl.pallas_call(
        finish_kernel,
        out_shape=(
            jax.ShapeDtypeStruct((N, trailing.shape[1]), F32),
            jax.ShapeDtypeStruct(trailing.shape, F32),
        ),
        in_specs=[VMEM] * 8,
        out_specs=(VMEM, VMEM),
        compiler_params=PARAMS,
        name="finish",
    )(inverse, kept, other, *blocks, trailing)


def paired(x, k):
    groups = lax.axis_size("grp")
    return x + lax.ppermute(x, "grp", [(g, g ^ k) for g in range(groups)])


def on_device(panel_block, trailing):
    along_x = [[z * X + x for x in range(X)] for z in range(Z)]
    along_z = [[z * X + x for z in range(Z)] for x in range(X)]
    rows = sent_to_all(panel_block, "dev", along_z).reshape(-1, N)

    own = gram_shares(rows)
    share = lax.all_to_all(own, "dev", 0, 0, axis_index_groups=along_x, tiled=True).sum(0)
    rows, _ = lax.optimization_barrier((rows, own))
    blocks = [rows]
    for k in range(1, X):
        moves = [(z * X + x, z * X + (x + k) % X) for z in range(Z) for x in range(X)]
        blocks.append(lax.ppermute(rows, "dev", moves))
    share = share + swapped(share)
    blocks[0], _ = lax.optimization_barrier((blocks[0], share))
    share = sent_to_all(share, "grp").sum(0)

    kept, given = cross_halves(blocks, trailing)
    kept = paired(kept + swapped(given), 1)
    share, kept = lax.optimization_barrier((share, kept))
    shares = sent_to_all(share, "dev")
    kept = paired(paired(kept, 2), 4)
    triangle, inverse = factor(shares, kept)
    projected, remainder = finish(inverse, kept, swapped(kept), blocks, trailing)
    return (triangle, projected, remainder)


def solution(mesh):
    placed = (P(("half", "grp", "dev"), None), P(("half", "grp"), "dev"))
    return jax.shard_map(
        on_device,
        mesh=mesh,
        in_specs=placed,
        out_specs=(P(), P(None, "dev"), P(("half", "grp"), "dev")),
        check_vma=False,
    )
```

```python
import jax
import jax.numpy as jnp
from jax import lax
from jax.experimental import pallas as pl
from jax.experimental.pallas import tpu as pltpu
from jax.sharding import PartitionSpec as P

N = 512
B = 128
V = 8
NB = N // B
NP = B // V
X = 4
Z = 8
PARTS = 4
GROUP = 8
SHARE_ROWS = B // X
HI = lax.Precision.HIGHEST
F32 = jnp.float32
BF16 = jnp.bfloat16
VMEM = pl.BlockSpec(memory_space=pltpu.VMEM)
PARAMS = pltpu.CompilerParams(vmem_limit_bytes=16 * 2**20)


def mm(a, b, dims=((1,), (0,))):
    return lax.dot_general(a, b, (dims, ((), ())), precision=HI, preferred_element_type=F32)


def three(x):
    high = x.astype(BF16)
    rest = x - high.astype(F32)
    middle = rest.astype(BF16)
    return high, middle, (rest - middle.astype(F32)).astype(BF16)


def left(x, axis):
    h, m, l = three(x)
    return jnp.concatenate([h, h, m, m, h, l], axis)


def right(x, axis):
    h, m, l = three(x)
    return jnp.concatenate([h, m, h, m, l, h], axis)


def two(x):
    high = x.astype(BF16)
    return high, (x - high.astype(F32)).astype(BF16)


def left2(x, axis):
    h, l = two(x)
    return jnp.concatenate([h, h, l], axis)


def right2(x, axis):
    h, l = two(x)
    return jnp.concatenate([h, l, h], axis)


def dot(a, b, dims):
    return lax.dot_general(a, b, (dims, ((), ())), preferred_element_type=F32)


def across_lanes(v, c):
    return jnp.broadcast_to(v[:, c : c + 1], (V, B))


def across_rows(v, j):
    return jnp.broadcast_to(v[j : j + 1, :], (V, B))


def eliminated(x, m0, m1, j, keep):
    return jnp.where(keep, x, 0.0) - m0 * across_rows(x, j) - m1 * across_rows(x, j + 1)


def total(terms):
    while len(terms) > 1:
        terms = [terms[i] + terms[i + 1] for i in range(0, len(terms), 2)]
    return terms[0]


def factor_block(m):
    row = lax.broadcasted_iota(jnp.int32, (V, B), 0)
    lane = lax.broadcasted_iota(jnp.int32, (V, B), 1)
    ups, invs, b = [], [], None
    for p in range(NP):
        r0 = p * V
        mp = m[p]
        diag = (lane >= r0) & (lane < r0 + V)
        eye = (lane == row + r0).astype(F32)
        more = p + 1 < NP
        if b is None:
            b = [across_lanes(mp, r0 + j) for j in range(V)]
        ahead = [across_lanes(mp, r0 + V + j) for j in range(V)] if more else []
        low, low_e, full = mp, eye, jnp.where(diag, eye, mp)
        dv = jnp.ones((V, B), F32)
        for j in range(0, V, 2):
            d, x, c = across_rows(b[j], j), across_rows(b[j], j + 1), across_rows(b[j + 1], j + 1)
            det = d * c - x * x
            over_det, over_d = 1.0 / det, 1.0 / d
            u0, u1 = b[j] * c - b[j + 1] * x, b[j + 1] * d - b[j] * x
            first, second, below = row == j, row == j + 1, row > j + 1
            keep = ~(first | second)
            m0 = jnp.where(first, -c, jnp.where(second, x, u0)) * over_det
            m1 = jnp.where(first, x, jnp.where(second, -d, u1)) * over_det
            for k in range(j + 2, V):
                b[k] = eliminated(b[k], m0, m1, j, keep)
            ahead = [eliminated(n, m0, m1, j, keep) for n in ahead]
            l0 = jnp.where(below, m0, jnp.where(second, x * over_d, 0.0))
            l1 = jnp.where(below, m1, 0.0)
            low = low - l0 * across_rows(low, j) - l1 * across_rows(low, j + 1)
            low_e = low_e - l0 * across_rows(low_e, j) - l1 * across_rows(low_e, j + 1)
            full = eliminated(full, m0, m1, j, keep)
            dv = jnp.where(first, d, jnp.where(second, det * over_d, dv))
        rs = lax.rsqrt(dv)
        ups.append(jnp.where(lane >= row + r0, low * rs, 0.0))
        invs.append(jnp.where(lane <= row + r0, jnp.where(diag, low_e, low) * rs, 0.0))
        if not more:
            break
        end = (p // GROUP + 1) * GROUP
        here = [across_lanes(m[p + 1], r0 + j) for j in range(V)]
        b = [
            across_lanes(m[p + 1], r0 + V + k) - total([here[j] * across_rows(ahead[k], j) for j in range(V)])
            for k in range(V)
        ]
        f = [across_rows(full, j) for j in range(V)]
        for q in range(p + 1, min(end + 1, NP)):
            old = m[q]
            m[q] = jnp.where(diag, 0.0, old) - total([across_lanes(old, r0 + j) * f[j] for j in range(V)])
        if p + 1 == end and end + 1 < NP:
            u, w = jnp.concatenate(ups[-GROUP:], 0), jnp.concatenate(invs[-GROUP:], 0)
            inverse_lanes = lax.broadcasted_iota(jnp.int32, u.shape, 1) < end * V
            update = dot(left(u, 0), right(jnp.where(inverse_lanes, w, u), 0), ((0,), (0,)))
            done = (lane >= (end - GROUP) * V) & (lane < end * V)
            for q in range(end + 1, NP):
                m[q] = jnp.where(done, 0.0, m[q]) - update[q * V : (q + 1) * V, :]
    return jnp.concatenate(ups, 0), jnp.concatenate(invs, 0)


def tile(g_ref, block, t):
    s = block * SHARE_ROWS + t % 4 * V
    return g_ref[s // 40 * X + t // 4, s % 40 : s % 40 + V, :]


def factor_kernel(g_ref, after_ref, r_ref, w_ref, end_ref, m_ref):
    block = 0
    for i in range(NB):
        for j in range(i, NB):
            for t in range(NP):
                m_ref[i * B + V * t : i * B + V * (t + 1), j * B : (j + 1) * B] = tile(g_ref, block, t)
            block += 1
    for k in range(NB):
        o = k * B
        e = o + B
        f = e + B
        u, v = factor_block([m_ref[o + V * i : o + V * (i + 1), o:e] for i in range(NP)])
        v_left = left(v, 1)
        r_ref[o:e, o:e] = u
        w_ref[o:e, o:e] = v
        if e < N:
            ps = dot(v_left, right(m_ref[o:e, e:], 0), ((1,), (0,)))
            r_ref[o:e, e:] = ps
            w_ref[o:e, e:] = jnp.zeros((B, N - e), F32)
            p_left, p_right = left(ps, 0), right(ps, 0)
            m_ref[e:f, e:] = m_ref[e:f, e:] - dot(p_left[:, :B], p_right, ((0,), (0,)))
            if f < N:
                m_ref[f:, f:] = m_ref[f:, f:] - dot(p_left[:, B:], p_right[:, B:], ((0,), (0,)))
        if k:
            wl = dot(v_left, right(m_ref[o:e, :o], 0), ((1,), (0,)))
            w_ref[o:e, :o] = wl
            r_ref[o:e, :o] = jnp.zeros((B, o), F32)
        if e < N:
            if k:
                m_ref[e:, :o] = m_ref[e:, :o] - dot(p_left, right(wl, 0), ((0,), (0,)))
            m_ref[e:, o:e] = -dot(p_left, right(v, 0), ((0,), (0,)))
    end_ref[...] = jnp.zeros_like(end_ref)


def factor(shares, after):
    out = jax.ShapeDtypeStruct((N, N), F32)
    return pl.pallas_call(
        factor_kernel,
        out_shape=(out, out, jax.ShapeDtypeStruct((V, B), F32)),
        scratch_shapes=[pltpu.VMEM((N, N), F32)],
        in_specs=[VMEM, pl.BlockSpec(memory_space=pl.ANY)],
        out_specs=(VMEM, VMEM, VMEM),
        compiler_params=PARAMS,
        cost_estimate=pl.CostEstimate(flops=20_000_000_000, bytes_accessed=3 * 2**20, transcendentals=0),
        name="factor",
    )(shares, after)


def sent_to_all(x, axis, groups=None):
    size = len(groups[0]) if groups else lax.axis_size(axis)
    copies = jnp.broadcast_to(x[None], (size, *x.shape))
    return lax.all_to_all(copies, axis, 0, 0, axis_index_groups=groups, tiled=True)


def swapped(x):
    return lax.ppermute(x, "half", [(0, 1), (1, 0)])


def gram_kernel(p_ref, own_ref, t_ref):
    first = lax.axis_index("dev") % X * SHARE_ROWS
    for i in range(NB):
        t_ref[i * B : (i + 1) * B, :] = p_ref[:, i * B : (i + 1) * B].T
    left = jnp.concatenate([t_ref[pl.ds(pl.multiple_of(i * B + first, SHARE_ROWS), SHARE_ROWS), :] for i in range(NB)], 0)
    g = mm(left, p_ref[...])
    block = 0
    for i in range(NB):
        for j in range(i, NB):
            for t in range(SHARE_ROWS // V):
                s, row = block * SHARE_ROWS + t * V, i * SHARE_ROWS + t * V
                own_ref[s // 40, s % 40 : s % 40 + V, :] = g[row : row + V, j * B : (j + 1) * B]
            block += 1


def gram_shares(rows):
    return pl.pallas_call(
        gram_kernel,
        out_shape=jax.ShapeDtypeStruct((Z, 40, B), F32),
        scratch_shapes=[pltpu.VMEM((N, rows.shape[0]), F32)],
        in_specs=[VMEM],
        out_specs=VMEM,
        compiler_params=PARAMS,
        name="gram",
    )(rows)


def cross_kernel(p_ref, t_ref, kept_ref, given_ref):
    rows = p_ref.shape[0] // PARTS
    product = None
    for i in range(PARTS):
        here = slice(i * rows, (i + 1) * rows)
        part = dot(left2(t_ref[here, :].T, 1), right2(p_ref[here, :], 0), ((1,), (0,)))
        product = part if product is None else product + part
    first = lax.axis_index("half") == 0
    low, high = product[:, : N // 2], product[:, N // 2 :]
    kept_ref[...] = jnp.where(first, low, high)
    given_ref[...] = jnp.where(first, high, low)


def cross_halves(panel_group, trailing):
    out = jax.ShapeDtypeStruct((trailing.shape[1], N // 2), F32)
    return pl.pallas_call(
        cross_kernel,
        out_shape=(out, out),
        in_specs=[VMEM] * 2,
        out_specs=(VMEM,) * 2,
        compiler_params=PARAMS,
        cost_estimate=pl.CostEstimate(flops=2_000_000_000, bytes_accessed=3 * 2**20, transcendentals=0),
        name="cross",
    )(panel_group, trailing)


def finish_kernel(w_ref, kept_ref, other_ref, p_ref, t_ref, end_ref, y_ref, r_ref):
    first = lax.axis_index("half") == 0
    kept, other = kept_ref[...], other_ref[...]
    cross = jnp.concatenate([jnp.where(first, kept, other), jnp.where(first, other, kept)], 1)
    w = w_ref[...]
    projected = dot(left2(cross, 1), right2(w, 1), ((1,), (1,)))
    y_ref[...] = projected.T
    solved = right2(dot(left2(projected, 1), right2(w, 0), ((1,), (0,))), 1)
    r_ref[...] = t_ref[...] - dot(left2(p_ref[...], 1), solved, ((1,), (1,)))


def finish(inverse, kept, other, panel_group, trailing, end):
    return pl.pallas_call(
        finish_kernel,
        out_shape=(
            jax.ShapeDtypeStruct((N, trailing.shape[1]), F32),
            jax.ShapeDtypeStruct(trailing.shape, F32),
        ),
        in_specs=[VMEM] * 6,
        out_specs=(VMEM, VMEM),
        compiler_params=PARAMS,
        name="finish",
    )(inverse, kept, other, panel_group, trailing, end)


def on_device(panel_block, trailing):
    along_x = [[z * X + x for x in range(X)] for z in range(Z)]
    along_z = [[z * X + x for z in range(Z)] for x in range(X)]
    groups = lax.axis_size("grp")
    alternate = [list(range(first, groups, 2)) for first in range(2)]
    rows = sent_to_all(panel_block, "dev", along_x).reshape(-1, N)
    panel_group = lax.all_gather(rows, "dev", axis=0, axis_index_groups=along_z, tiled=True)

    own = gram_shares(rows)
    share = lax.all_to_all(own, "dev", 0, 0, axis_index_groups=along_z, tiled=True).sum(0)
    share = share + swapped(share)
    share = sent_to_all(share, "grp").sum(0)
    shares = sent_to_all(share, "dev")

    panel_group, _ = lax.optimization_barrier((panel_group, share))
    kept, given = cross_halves(panel_group, trailing)
    kept = kept + swapped(given)
    kept = kept + lax.ppermute(kept, "grp", [(g, g ^ 1) for g in range(groups)])

    triangle, inverse, end = factor(shares, kept)
    kept = sent_to_all(kept, "grp", alternate).sum(0)
    kept, end = lax.optimization_barrier((kept, end))
    other = swapped(kept)
    projected, remainder = finish(inverse, kept, other, panel_group, trailing, end)
    return (triangle, projected, remainder)


def solution(mesh):
    placed = (P(("half", "grp", "dev"), None), P(("half", "grp"), "dev"))
    return jax.shard_map(
        on_device,
        mesh=mesh,
        in_specs=placed,
        out_specs=(P(), P(None, "dev"), P(("half", "grp"), "dev")),
        check_vma=False,
    )
```

```python
import jax
import jax.numpy as jnp
from jax import lax
from jax.experimental import pallas as pl
from jax.experimental.pallas import tpu as pltpu
from jax.sharding import PartitionSpec as P

N = 512
B = 128
V = 8
NB = N // B
NP = B // V
X = 4
Z = 8
PARTS = 4
GROUP = 8
SHARE_ROWS = B // X
HI = lax.Precision.HIGHEST
F32 = jnp.float32
BF16 = jnp.bfloat16
VMEM = pl.BlockSpec(memory_space=pltpu.VMEM)
PARAMS = pltpu.CompilerParams(vmem_limit_bytes=16 * 2**20)


def mm(a, b, dims=((1,), (0,))):
    return lax.dot_general(a, b, (dims, ((), ())), precision=HI, preferred_element_type=F32)


def three(x):
    high = x.astype(BF16)
    rest = x - high.astype(F32)
    middle = rest.astype(BF16)
    return high, middle, (rest - middle.astype(F32)).astype(BF16)


def left(x, axis):
    h, m, l = three(x)
    return jnp.concatenate([h, h, m, m, h, l], axis)


def right(x, axis):
    h, m, l = three(x)
    return jnp.concatenate([h, m, h, m, l, h], axis)


def two(x):
    high = x.astype(BF16)
    return high, (x - high.astype(F32)).astype(BF16)


def left2(x, axis):
    h, l = two(x)
    return jnp.concatenate([h, h, l], axis)


def right2(x, axis):
    h, l = two(x)
    return jnp.concatenate([h, l, h], axis)


def dot(a, b, dims):
    return lax.dot_general(a, b, (dims, ((), ())), preferred_element_type=F32)


def across_lanes(v, c):
    return jnp.broadcast_to(v[:, c : c + 1], (V, B))


def across_rows(v, j):
    return jnp.broadcast_to(v[j : j + 1, :], (V, B))


def eliminated(x, m0, m1, j, keep):
    return jnp.where(keep, x, 0.0) - m0 * across_rows(x, j) - m1 * across_rows(x, j + 1)


def total(terms):
    while len(terms) > 1:
        terms = [terms[i] + terms[i + 1] for i in range(0, len(terms), 2)]
    return terms[0]


def factor_block(m):
    row = lax.broadcasted_iota(jnp.int32, (V, B), 0)
    lane = lax.broadcasted_iota(jnp.int32, (V, B), 1)
    ups, invs, b = [], [], None
    for p in range(NP):
        r0 = p * V
        mp = m[p]
        diag = (lane >= r0) & (lane < r0 + V)
        eye = (lane == row + r0).astype(F32)
        more = p + 1 < NP
        if b is None:
            b = [across_lanes(mp, r0 + j) for j in range(V)]
        ahead = [across_lanes(mp, r0 + V + j) for j in range(V)] if more else []
        low, low_e, full = mp, eye, jnp.where(diag, eye, mp)
        dv = jnp.ones((V, B), F32)
        for j in range(0, V, 2):
            d, x, c = across_rows(b[j], j), across_rows(b[j], j + 1), across_rows(b[j + 1], j + 1)
            det = d * c - x * x
            over_det, over_d = 1.0 / det, 1.0 / d
            u0, u1 = b[j] * c - b[j + 1] * x, b[j + 1] * d - b[j] * x
            first, second, below = row == j, row == j + 1, row > j + 1
            keep = ~(first | second)
            m0 = jnp.where(first, -c, jnp.where(second, x, u0)) * over_det
            m1 = jnp.where(first, x, jnp.where(second, -d, u1)) * over_det
            for k in range(j + 2, V):
                b[k] = eliminated(b[k], m0, m1, j, keep)
            ahead = [eliminated(n, m0, m1, j, keep) for n in ahead]
            l0 = jnp.where(below, m0, jnp.where(second, x * over_d, 0.0))
            l1 = jnp.where(below, m1, 0.0)
            low = low - l0 * across_rows(low, j) - l1 * across_rows(low, j + 1)
            low_e = low_e - l0 * across_rows(low_e, j) - l1 * across_rows(low_e, j + 1)
            full = eliminated(full, m0, m1, j, keep)
            dv = jnp.where(first, d, jnp.where(second, det * over_d, dv))
        rs = lax.rsqrt(dv)
        ups.append(jnp.where(lane >= row + r0, low * rs, 0.0))
        invs.append(jnp.where(lane <= row + r0, jnp.where(diag, low_e, low) * rs, 0.0))
        if not more:
            break
        end = (p // GROUP + 1) * GROUP
        here = [across_lanes(m[p + 1], r0 + j) for j in range(V)]
        b = [
            across_lanes(m[p + 1], r0 + V + k) - total([here[j] * across_rows(ahead[k], j) for j in range(V)])
            for k in range(V)
        ]
        f = [across_rows(full, j) for j in range(V)]
        for q in range(p + 1, min(end + 1, NP)):
            old = m[q]
            m[q] = jnp.where(diag, 0.0, old) - total([across_lanes(old, r0 + j) * f[j] for j in range(V)])
        if p + 1 == end and end + 1 < NP:
            u, w = jnp.concatenate(ups[-GROUP:], 0), jnp.concatenate(invs[-GROUP:], 0)
            inverse_lanes = lax.broadcasted_iota(jnp.int32, u.shape, 1) < end * V
            update = dot(left(u, 0), right(jnp.where(inverse_lanes, w, u), 0), ((0,), (0,)))
            done = (lane >= (end - GROUP) * V) & (lane < end * V)
            for q in range(end + 1, NP):
                m[q] = jnp.where(done, 0.0, m[q]) - update[q * V : (q + 1) * V, :]
    return jnp.concatenate(ups, 0), jnp.concatenate(invs, 0)


def tile(g_ref, block, t):
    s = block * SHARE_ROWS + t % 4 * V
    return g_ref[s // 40 * X + t // 4, s % 40 : s % 40 + V, :]


def factor_kernel(g_ref, after_ref, r_ref, w_ref, end_ref, m_ref):
    block = 0
    for i in range(NB):
        for j in range(i, NB):
            for t in range(NP):
                m_ref[i * B + V * t : i * B + V * (t + 1), j * B : (j + 1) * B] = tile(g_ref, block, t)
            block += 1
    on_diagonal = lax.broadcasted_iota(jnp.int32, (B, B), 0) == lax.broadcasted_iota(jnp.int32, (B, B), 1)
    diagonals = [jnp.where(on_diagonal, m_ref[i * B : (i + 1) * B, i * B : (i + 1) * B], 0.0) for i in range(NB)]
    scale = lax.rsqrt(jnp.concatenate([jnp.sum(d, 0, keepdims=True) for d in diagonals], 1))
    for i in range(NB):
        here = slice(i * B, (i + 1) * B)
        m_ref[here, i * B :] = m_ref[here, i * B :] * lax.rsqrt(jnp.sum(diagonals[i], 1, keepdims=True)) * scale[:, i * B :]
    for k in range(NB):
        o = k * B
        e = o + B
        f = e + B
        u, v = factor_block([m_ref[o + V * i : o + V * (i + 1), o:e] for i in range(NP)])
        v_left = left(v, 1)
        r_ref[o:e, o:e] = u
        w_ref[o:e, o:e] = v
        if e < N:
            ps = dot(v_left, right(m_ref[o:e, e:], 0), ((1,), (0,)))
            r_ref[o:e, e:] = ps
            w_ref[o:e, e:] = jnp.zeros((B, N - e), F32)
            p_left, p_right = left(ps, 0), right(ps, 0)
            m_ref[e:f, e:] = m_ref[e:f, e:] - dot(p_left[:, :B], p_right, ((0,), (0,)))
            if f < N:
                m_ref[f:, f:] = m_ref[f:, f:] - dot(p_left[:, B:], p_right[:, B:], ((0,), (0,)))
        if k:
            wl = dot(v_left, right(m_ref[o:e, :o], 0), ((1,), (0,)))
            w_ref[o:e, :o] = wl
            r_ref[o:e, :o] = jnp.zeros((B, o), F32)
        if e < N:
            if k:
                m_ref[e:, :o] = m_ref[e:, :o] - dot(p_left, right(wl, 0), ((0,), (0,)))
            m_ref[e:, o:e] = -dot(p_left, right(v, 0), ((0,), (0,)))
    r_ref[...] = r_ref[...] * (1.0 / scale)
    w_ref[...] = w_ref[...] * scale
    end_ref[...] = jnp.zeros_like(end_ref)


def factor(shares, after):
    out = jax.ShapeDtypeStruct((N, N), F32)
    return pl.pallas_call(
        factor_kernel,
        out_shape=(out, out, jax.ShapeDtypeStruct((V, B), F32)),
        scratch_shapes=[pltpu.VMEM((N, N), F32)],
        in_specs=[VMEM, pl.BlockSpec(memory_space=pl.ANY)],
        out_specs=(VMEM, VMEM, VMEM),
        compiler_params=PARAMS,
        cost_estimate=pl.CostEstimate(flops=20_000_000_000, bytes_accessed=3 * 2**20, transcendentals=0),
        name="factor",
    )(shares, after)


def sent_to_all(x, axis, groups=None):
    size = len(groups[0]) if groups else lax.axis_size(axis)
    copies = jnp.broadcast_to(x[None], (size, *x.shape))
    return lax.all_to_all(copies, axis, 0, 0, axis_index_groups=groups, tiled=True)


def swapped(x):
    return lax.ppermute(x, "half", [(0, 1), (1, 0)])


def gram_kernel(p_ref, own_ref, t_ref):
    first = lax.axis_index("dev") % X * SHARE_ROWS
    for i in range(NB):
        t_ref[i * B : (i + 1) * B, :] = p_ref[:, i * B : (i + 1) * B].T
    left = jnp.concatenate([t_ref[pl.ds(pl.multiple_of(i * B + first, SHARE_ROWS), SHARE_ROWS), :] for i in range(NB)], 0)
    g = mm(left, p_ref[...])
    block = 0
    for i in range(NB):
        for j in range(i, NB):
            for t in range(SHARE_ROWS // V):
                s, row = block * SHARE_ROWS + t * V, i * SHARE_ROWS + t * V
                own_ref[s // 40, s % 40 : s % 40 + V, :] = g[row : row + V, j * B : (j + 1) * B]
            block += 1


def gram_shares(rows):
    return pl.pallas_call(
        gram_kernel,
        out_shape=jax.ShapeDtypeStruct((Z, 40, B), F32),
        scratch_shapes=[pltpu.VMEM((N, rows.shape[0]), F32)],
        in_specs=[VMEM],
        out_specs=VMEM,
        compiler_params=PARAMS,
        name="gram",
    )(rows)


def cross_kernel(p_ref, t_ref, kept_ref, given_ref):
    rows = p_ref.shape[0] // PARTS
    product = None
    for i in range(PARTS):
        here = slice(i * rows, (i + 1) * rows)
        part = dot(left2(t_ref[here, :].T, 1), right2(p_ref[here, :], 0), ((1,), (0,)))
        product = part if product is None else product + part
    first = lax.axis_index("half") == 0
    low, high = product[:, : N // 2], product[:, N // 2 :]
    kept_ref[...] = jnp.where(first, low, high)
    given_ref[...] = jnp.where(first, high, low)


def cross_halves(panel_group, trailing):
    out = jax.ShapeDtypeStruct((trailing.shape[1], N // 2), F32)
    return pl.pallas_call(
        cross_kernel,
        out_shape=(out, out),
        in_specs=[VMEM] * 2,
        out_specs=(VMEM,) * 2,
        compiler_params=PARAMS,
        cost_estimate=pl.CostEstimate(flops=2_000_000_000, bytes_accessed=3 * 2**20, transcendentals=0),
        name="cross",
    )(panel_group, trailing)


def finish_kernel(w_ref, kept_ref, other_ref, p_ref, t_ref, end_ref, y_ref, r_ref):
    first = lax.axis_index("half") == 0
    kept, other = kept_ref[...], other_ref[...]
    cross = jnp.concatenate([jnp.where(first, kept, other), jnp.where(first, other, kept)], 1)
    w = w_ref[...]
    projected = dot(left2(cross, 1), right2(w, 1), ((1,), (1,)))
    y_ref[...] = projected.T
    solved = right2(dot(left2(projected, 1), right2(w, 0), ((1,), (0,))), 1)
    r_ref[...] = t_ref[...] - dot(left2(p_ref[...], 1), solved, ((1,), (1,)))


def finish(inverse, kept, other, panel_group, trailing, end):
    return pl.pallas_call(
        finish_kernel,
        out_shape=(
            jax.ShapeDtypeStruct((N, trailing.shape[1]), F32),
            jax.ShapeDtypeStruct(trailing.shape, F32),
        ),
        in_specs=[VMEM] * 6,
        out_specs=(VMEM, VMEM),
        compiler_params=PARAMS,
        name="finish",
    )(inverse, kept, other, panel_group, trailing, end)


def on_device(panel_block, trailing):
    along_x = [[z * X + x for x in range(X)] for z in range(Z)]
    along_z = [[z * X + x for z in range(Z)] for x in range(X)]
    groups = lax.axis_size("grp")
    alternate = [list(range(first, groups, 2)) for first in range(2)]
    rows = sent_to_all(panel_block, "dev", along_x).reshape(-1, N)
    panel_group = lax.all_gather(rows, "dev", axis=0, axis_index_groups=along_z, tiled=True)

    own = gram_shares(rows)
    share = lax.all_to_all(own, "dev", 0, 0, axis_index_groups=along_z, tiled=True).sum(0)
    share = share + swapped(share)
    share = sent_to_all(share, "grp").sum(0)
    shares = sent_to_all(share, "dev")

    panel_group, _ = lax.optimization_barrier((panel_group, share))
    kept, given = cross_halves(panel_group, trailing)
    kept = kept + swapped(given)
    kept = kept + lax.ppermute(kept, "grp", [(g, g ^ 1) for g in range(groups)])

    triangle, inverse, end = factor(shares, kept)
    kept = sent_to_all(kept, "grp", alternate).sum(0)
    kept, end = lax.optimization_barrier((kept, end))
    other = swapped(kept)
    projected, remainder = finish(inverse, kept, other, panel_group, trailing, end)
    return (triangle, projected, remainder)


def solution(mesh):
    placed = (P(("half", "grp", "dev"), None), P(("half", "grp"), "dev"))
    return jax.shard_map(
        on_device,
        mesh=mesh,
        in_specs=placed,
        out_specs=(P(), P(None, "dev"), P(("half", "grp"), "dev")),
        check_vma=False,
    )
```
